32 devices in a mesh: pre: 16 (over z, x, core), br: 2 (over y).
Axes of the slice: x: 2, y: 2, z: 4, core: 2. Of those that a mesh axis runs over, the one named last changes fastest.
Arguments:
- prompt_query: bfloat16 [1024, 8192], P('pre', 'br'), may hold values from -6 to 6
- prompt_key_rows: bfloat16 [1024, 1024], P('pre', 'br'), may hold values from -6 to 6
- prompt_value_rows: bfloat16 [1024, 1024], P('pre', 'br'), may hold values from -6 to 6
- prompt_grad_out: bfloat16 [1024, 8192], P('pre', 'br'), may hold values from -6 to 6
- prompt_lse: float32 [1024, 64], P('pre', 'br'), may hold values from 3 to 7
- prompt_delta: float32 [1024, 64], P('pre', 'br'), may hold values from -48 to 48
- resp_query: bfloat16 [2048, 8192], P(('pre', 'br')), may hold values from -6 to 6
- response_key_rows: bfloat16 [2048, 1024], P(('pre', 'br')), may hold values from -6 to 6
- response_value_rows: bfloat16 [2048, 1024], P(('pre', 'br')), may hold values from -6 to 6
- resp_grad_out: bfloat16 [2048, 8192], P(('pre', 'br')), may hold values from -6 to 6
- resp_lse: float32 [2048, 64], P(('pre', 'br')), may hold values from 3 to 7
- resp_delta: float32 [2048, 64], P(('pre', 'br')), may hold values from -48 to 48
- resp_segment: int32 [2048], P(('pre', 'br')), may hold values from -1 to 2047, as said below
Outputs:
- prompt_dq: bfloat16 [1024, 8192], P('pre', 'br')
- prompt_dk: bfloat16 [1024, 1024], P('pre', 'br')
- prompt_dv: bfloat16 [1024, 1024], P('pre', 'br')
- resp_dq: bfloat16 [2048, 8192], P(('pre', 'br'))
- response_key_gradient: bfloat16 [2048, 1024], P(('pre', 'br'))
- response_value_gradient: bfloat16 [2048, 1024], P(('pre', 'br'))
The draws below stay inside these ranges and needn't reach their ends.
Inputs may be any that keep to these rules, and one draw needn't show every extreme that they name: `resp_segment`: each response occupies consecutive rows inside one aligned block of 64 rows and is named by the index of its first row; unused rows, which hold -1, stand at the end of a block; every block uses at least half of its rows, and block 0 holds one response of 64 rows.
All inputs are finite; a program needn't handle non-finite values.
Results may differ from the reference program's by a relative error of at most 0.007.
Values may be sent and summed in bfloat16 or wider, within the bound.
A program may use at most 128 MiB of HBM per device.

```python
import jax
import jax.numpy as jnp
from jax import lax

HQ = 64
KEY_VALUE_HEADS = 8
HEAD_SIZE = 128
P_DEV = 64
RB = 64
PROMPT_LENGTH = 1024
RESPONSE_ROWS = 2048
N_PRE = 16
N_BR = 2


def draw_resp_segment(key, part):
    key = jax.random.fold_in(key, 11)
    key_fill, key_start = jax.random.split(key)
    block_total = RESPONSE_ROWS // RB
    block_ids = jnp.arange(block_total, dtype=jnp.int32)[:, None]
    row_index = jnp.arange(RB, dtype=jnp.int32)[None, :]
    fills = jax.random.randint(key_fill, (block_total, 1), RB // 2, RB + 1).astype(jnp.int32)
    fills = jnp.where(block_ids == 0, RB, fills)
    starts = jax.random.randint(key_start, (block_total, RB), 0, max(RB // 2, 2)) == 0
    starts = starts & (block_ids != 0) | (row_index == 0)
    first_rows = block_ids * RB + row_index
    markers = jnp.where(starts, first_rows, -1)
    segment = lax.cummax(markers, axis=1)
    segment = jnp.where(row_index < fills, segment, -1)
    return segment.reshape(RESPONSE_ROWS).astype(jnp.int32)


def shard_levels(rng, shape, cuts, low, high):
    level = 1.0
    for position, blocks in cuts:
        draws = jax.random.uniform(jax.random.fold_in(jax.random.fold_in(rng, 6), position), (blocks,), jnp.float32, low / len(cuts), high / len(cuts))
        level = level * jnp.repeat(jnp.exp(draws), shape[position] // blocks).reshape((-1,) + (1,) * (len(shape) - 1 - position))
    return level


def bell_draw(stream_key, shape, scale, reach, shards=(), kind=jnp.bfloat16):
    gain = shard_levels(stream_key, shape, shards, -0.22, 0.18) if shards else 1.0
    drawn = jax.random.normal(stream_key, shape, jnp.float32) * scale * gain
    return jnp.minimum(jnp.maximum(drawn, -reach), reach).astype(kind)


def setup_inputs(seed: int = 0) -> dict:
    key_list = jax.random.split(jax.random.key(seed), 14)
    return {
        "prompt_query": bell_draw(key_list[0], (PROMPT_LENGTH, HQ * HEAD_SIZE), 1.0, 6.0, ((0, 16), (1, 2))),
        "prompt_key_rows": bell_draw(key_list[1], (PROMPT_LENGTH, KEY_VALUE_HEADS * HEAD_SIZE), 1.0, 6.0, ((0, 16), (1, 2))),
        "prompt_value_rows": bell_draw(key_list[2], (PROMPT_LENGTH, KEY_VALUE_HEADS * HEAD_SIZE), 1.0, 6.0, ((0, 16), (1, 2))),
        "prompt_grad_out": bell_draw(key_list[3], (PROMPT_LENGTH, HQ * HEAD_SIZE), 1.0, 6.0, ((0, 16), (1, 2))),
        "prompt_lse": jnp.clip(3.0 + 4.0 * jax.random.uniform(key_list[4], (PROMPT_LENGTH, HQ), jnp.float32) ** shard_levels(key_list[4], (PROMPT_LENGTH, HQ), ((0, 16), (1, 2)), -0.2, 0.2), 3.0, 7.0),
        "prompt_delta": bell_draw(key_list[5], (PROMPT_LENGTH, HQ), 8.0, 48.0, ((0, 16), (1, 2)), jnp.float32),
        "resp_query": bell_draw(key_list[6], (RESPONSE_ROWS, HQ * HEAD_SIZE), 1.0, 6.0, ((0, 32),)),
        "response_key_rows": bell_draw(key_list[7], (RESPONSE_ROWS, KEY_VALUE_HEADS * HEAD_SIZE), 1.0, 6.0, ((0, 32),)),
        "response_value_rows": bell_draw(key_list[8], (RESPONSE_ROWS, KEY_VALUE_HEADS * HEAD_SIZE), 1.0, 6.0, ((0, 32),)),
        "resp_grad_out": bell_draw(key_list[9], (RESPONSE_ROWS, HQ * HEAD_SIZE), 1.0, 6.0, ((0, 32),)),
        "resp_lse": jnp.clip(3.0 + 4.0 * jax.random.uniform(key_list[10], (RESPONSE_ROWS, HQ), jnp.float32) ** shard_levels(key_list[10], (RESPONSE_ROWS, HQ), ((0, 32),), -0.2, 0.2), 3.0, 7.0),
        "resp_delta": bell_draw(key_list[11], (RESPONSE_ROWS, HQ), 8.0, 48.0, ((0, 32),), jnp.float32),
        "resp_segment": draw_resp_segment(jax.random.fold_in(key_list[13], 71), 0),
    }


def attend(query, grad_out, log_norm, row_term, keys, values, allowed):
    row_count = query.shape[0]
    key_count = keys.shape[0]
    groups = keys.shape[1] // HEAD_SIZE
    ratio = query.shape[1] // (groups * HEAD_SIZE)
    scaling = HEAD_SIZE ** -0.5
    query_heads = query.astype(jnp.float32).reshape(row_count, groups, ratio, HEAD_SIZE)
    grad_heads = grad_out.astype(jnp.float32).reshape(row_count, groups, ratio, HEAD_SIZE)
    key_heads = keys.astype(jnp.float32).reshape(key_count, groups, HEAD_SIZE)
    value_heads = values.astype(jnp.float32).reshape(key_count, groups, HEAD_SIZE)
    norm_t = log_norm.reshape(row_count, groups, ratio).transpose(1, 2, 0)[..., None]
    term_t = row_term.reshape(row_count, groups, ratio).transpose(1, 2, 0)[..., None]
    scores = jnp.einsum('rgqd,ngd->gqrn', query_heads, key_heads) * scaling
    weights = jnp.where(allowed[None, None], jnp.exp(scores - norm_t), 0.0)
    dweights = jnp.einsum('rgqd,ngd->gqrn', grad_heads, value_heads)
    dscores = weights * (dweights - term_t)
    weights_b = lax.optimization_barrier(weights.astype(jnp.bfloat16)).astype(jnp.float32)
    dscores_b = lax.optimization_barrier(dscores.astype(jnp.bfloat16)).astype(jnp.float32)
    grad_v = jnp.einsum('gqrn,rgqd->ngd', weights_b, grad_heads)
    grad_k = jnp.einsum('gqrn,rgqd->ngd', dscores_b, query_heads) * scaling
    grad_q = jnp.einsum('gqrn,ngd->rgqd', dscores_b, key_heads) * scaling
    return grad_q.reshape(row_count, -1), grad_k.reshape(key_count, -1), grad_v.reshape(key_count, -1)


def own_mask(segment):
    index = jnp.arange(segment.shape[0], dtype=jnp.int32)
    same = segment[:, None] == segment[None, :]
    return same & (segment[:, None] >= 0) & (index[None, :] <= index[:, None])


def reference(prompt_query, prompt_key_rows, prompt_value_rows, prompt_grad_out, prompt_lse, prompt_delta, resp_query, response_key_rows, response_value_rows, resp_grad_out, resp_lse, resp_delta, resp_segment):
    prompt_pos = jnp.arange(PROMPT_LENGTH, dtype=jnp.int32)
    blank_slot = jnp.zeros((PROMPT_LENGTH, KEY_VALUE_HEADS * HEAD_SIZE), jnp.float32)

    def prompt_block(totals, block_index):
        first_row = (block_index * P_DEV).astype(jnp.int32)
        query = lax.dynamic_slice_in_dim(prompt_query, first_row, P_DEV, 0)
        grad_out = lax.dynamic_slice_in_dim(prompt_grad_out, first_row, P_DEV, 0)
        log_norm = lax.dynamic_slice_in_dim(prompt_lse, first_row, P_DEV, 0)
        row_term = lax.dynamic_slice_in_dim(prompt_delta, first_row, P_DEV, 0)
        row_pos = first_row + jnp.arange(P_DEV, dtype=jnp.int32)
        allowed = prompt_pos[None, :] <= row_pos[:, None]
        grad_q, grad_k, grad_v = attend(query, grad_out, log_norm, row_term, prompt_key_rows, prompt_value_rows, allowed)
        return (totals[0] + grad_k, totals[1] + grad_v), grad_q.astype(jnp.bfloat16)

    totals, prompt_blocks = lax.scan(prompt_block, (blank_slot, blank_slot), jnp.arange(N_PRE, dtype=jnp.int32))

    def resp_block(totals, block_index):
        first_row = (block_index * RB).astype(jnp.int32)
        query = lax.dynamic_slice_in_dim(resp_query, first_row, RB, 0)
        grad_out = lax.dynamic_slice_in_dim(resp_grad_out, first_row, RB, 0)
        log_norm = lax.dynamic_slice_in_dim(resp_lse, first_row, RB, 0)
        row_term = lax.dynamic_slice_in_dim(resp_delta, first_row, RB, 0)
        own_keys = lax.dynamic_slice_in_dim(response_key_rows, first_row, RB, 0)
        own_values = lax.dynamic_slice_in_dim(response_value_rows, first_row, RB, 0)
        segment = lax.dynamic_slice_in_dim(resp_segment, first_row, RB, 0)
        usable = jnp.broadcast_to((segment >= 0)[:, None], (RB, PROMPT_LENGTH))
        far_q, far_k, far_v = attend(query, grad_out, log_norm, row_term, prompt_key_rows, prompt_value_rows, usable)
        near_q, near_k, near_v = attend(query, grad_out, log_norm, row_term, own_keys, own_values, own_mask(segment))
        outputs = ((far_q + near_q).astype(jnp.bfloat16), near_k.astype(jnp.bfloat16), near_v.astype(jnp.bfloat16))
        return (totals[0] + far_k, totals[1] + far_v), outputs

    totals, response_block_list = lax.scan(resp_block, totals, jnp.arange(N_PRE * N_BR, dtype=jnp.int32))
    prompt_dq = prompt_blocks.reshape(PROMPT_LENGTH, HQ * HEAD_SIZE)
    resp_dq = response_block_list[0].reshape(RESPONSE_ROWS, HQ * HEAD_SIZE)
    response_key_gradient = response_block_list[1].reshape(RESPONSE_ROWS, KEY_VALUE_HEADS * HEAD_SIZE)
    response_value_gradient = response_block_list[2].reshape(RESPONSE_ROWS, KEY_VALUE_HEADS * HEAD_SIZE)
    return (prompt_dq, totals[0].astype(jnp.bfloat16), totals[1].astype(jnp.bfloat16), resp_dq, response_key_gradient, response_value_gradient)
```

```python
import functools

import jax
import jax.numpy as jnp
from jax import lax
from jax.experimental import pallas as pl
from jax.experimental.pallas import tpu as pltpu
from jax.sharding import PartitionSpec as P

HEAD = 128
SCALE = HEAD ** (-0.5)
LOG2E = 1.4426950408889634
F32 = jnp.float32
BF16 = jnp.bfloat16


def dot(a, b, ca, cb):
    return lax.dot_general(a, b, (((ca,), (cb,)), ((), ())), preferred_element_type=F32)


def stack_heads(block):
    ratio = block.shape[1] // HEAD
    return jnp.concatenate([block[:, h * HEAD : (h + 1) * HEAD] for h in range(ratio)], 0)


def spread_heads(dq_t, rows):
    dq = dq_t.T
    ratio = dq.shape[0] // rows
    return jnp.concatenate([dq[h * rows : (h + 1) * rows] for h in range(ratio)], 1)


def terms(k, v, q, go, norm, delta, bias):
    s = dot(k, q, 1, 1)
    z = s * (SCALE * LOG2E) - norm
    if bias is not None:
        z = z + bias
    w = jnp.exp2(z)
    ds = w * (dot(v, go, 1, 1) - delta)
    wb = w.astype(BF16)
    dsb = ds.astype(BF16)
    return dot(dsb, q, 1, 0) * SCALE, dot(wb, go, 1, 0), dot(k, dsb, 0, 0)


def attention_kernel(
    chunk_blocks,
    place,
    kv_ref,
    rq_ref,
    rgo_ref,
    rnorm_ref,
    rdelta_ref,
    bias_ref,
    rk_ref,
    rv_ref,
    pq_ref,
    pgo_ref,
    pnorm_ref,
    pdelta_ref,
    dkv_ref,
    rdq_ref,
    rdk_ref,
    rdv_ref,
    pdq_ref,
    racc,
    pacc,
):
    n_pre, _, _, block_rows, _ = kv_ref.shape
    group = pl.program_id(0)
    pre = place[0]
    per_br = place[2]
    mine = (group // per_br) == place[1]
    rows = rq_ref.shape[0]
    prow = pq_ref.shape[0]
    chunk = chunk_blocks * block_rows
    rq = stack_heads(rq_ref[...])
    rgo = stack_heads(rgo_ref[...])
    rnorm = rnorm_ref[0]
    rdelta = rdelta_ref[0]
    dk, dv, dq = terms(rk_ref[...], rv_ref[...], rq, rgo, rnorm, rdelta, bias_ref[...])
    rdk_ref[...] = dk.astype(BF16)
    rdv_ref[...] = dv.astype(BF16)
    racc[...] = dq

    @pl.when(mine)
    def _():
        pacc[...] = jnp.zeros_like(pacc)

    for c in range(n_pre // chunk_blocks):
        at = pl.ds(c * chunk_blocks, chunk_blocks)
        k = kv_ref[at, 0, 0].reshape(chunk, HEAD)
        v = kv_ref[at, 0, 1].reshape(chunk, HEAD)
        dk, dv, dq = terms(k, v, rq, rgo, rnorm, rdelta, None)
        racc[...] += dq
        with_prompt = mine & (c * chunk < (pre + 1) * prow)

        @pl.when(with_prompt)
        def _():
            pq = stack_heads(pq_ref[...])
            pgo = stack_heads(pgo_ref[...])
            key = lax.broadcasted_iota(jnp.int32, (chunk, pq.shape[0]), 0) + c * chunk
            row = lax.rem(lax.broadcasted_iota(jnp.int32, (chunk, pq.shape[0]), 1), prow)
            bias = jnp.where(key <= row + pre * prow, 0.0, -1e30)
            pdk, pdv, pdq = terms(k, v, pq, pgo, pnorm_ref[0], pdelta_ref[0], bias)
            pacc[...] += pdq
            dkv_ref[at, 0, 0] = (dk + pdk).reshape(chunk_blocks, block_rows, HEAD)
            dkv_ref[at, 0, 1] = (dv + pdv).reshape(chunk_blocks, block_rows, HEAD)

        @pl.when(jnp.logical_not(with_prompt))
        def _():
            dkv_ref[at, 0, 0] = dk.reshape(chunk_blocks, block_rows, HEAD)
            dkv_ref[at, 0, 1] = dv.reshape(chunk_blocks, block_rows, HEAD)

    rdq_ref[...] = (spread_heads(racc[...], rows) * SCALE).astype(BF16)

    @pl.when(mine)
    def _():
        pdq_ref[...] = (spread_heads(pacc[...], prow) * SCALE).astype(BF16)


def per_group(x, groups):
    rows, heads = x.shape
    return x.T.reshape(groups, 1, heads // groups * rows)


def local(
    n_pre,
    n_br,
    prompt_query,
    prompt_key_rows,
    prompt_value_rows,
    prompt_grad_out,
    prompt_lse,
    prompt_delta,
    resp_query,
    response_key_rows,
    response_value_rows,
    resp_grad_out,
    resp_lse,
    resp_delta,
    resp_segment,
):
    prow, cols = prompt_key_rows.shape
    rows, width = response_key_rows.shape
    groups = width // HEAD
    per_br = cols // HEAD
    ratio = resp_query.shape[1] // width
    wide = ratio * HEAD
    pre = lax.axis_index("pre").astype(jnp.int32)
    br = lax.axis_index("br").astype(jnp.int32)
    place = jnp.stack([pre, br, jnp.int32(per_br)])

    kv = jnp.stack([prompt_key_rows, prompt_value_rows])
    kv_all = lax.all_gather(kv, ("pre", "br"), axis=0, tiled=False)
    kv_all = kv_all.reshape(n_pre, n_br, 2, prow, cols)

    usable = (resp_segment >= 0)[:, None]
    rnorm = per_group(jnp.where(usable, resp_lse * LOG2E, 1e30), groups)
    rdelta = per_group(resp_delta, groups)
    pnorm = per_group(prompt_lse * LOG2E, per_br)
    pdelta = per_group(prompt_delta, per_br)
    index = jnp.arange(rows, dtype=jnp.int32)
    seen = (resp_segment[:, None] == resp_segment[None, :]) & (index[:, None] <= index[None, :])
    bias = jnp.tile(jnp.where(seen, 0.0, -1e30), (1, ratio))

    def kv_at(g, place):
        return (0, g // per_br, 0, 0, g % per_br)

    def prompt_g(g, place):
        return jnp.clip(g - place[1] * per_br, 0, per_br - 1)

    chunk_blocks = max(1, 256 // prow)
    col = lambda g, place: (0, g)
    pcol = lambda g, place: (0, prompt_g(g, place))
    lead = lambda g, place: (g, 0, 0)
    plead = lambda g, place: (prompt_g(g, place), 0, 0)
    dkv, rdq, rdk, rdv, pdq = pl.pallas_call(
        functools.partial(attention_kernel, chunk_blocks),
        grid_spec=pltpu.PrefetchScalarGridSpec(
            num_scalar_prefetch=1,
            grid=(groups,),
            in_specs=[
                pl.BlockSpec((n_pre, 1, 2, prow, HEAD), kv_at),
                pl.BlockSpec((rows, wide), col),
                pl.BlockSpec((rows, wide), col),
                pl.BlockSpec((1, 1, ratio * rows), lead),
                pl.BlockSpec((1, 1, ratio * rows), lead),
                pl.BlockSpec((rows, ratio * rows), lambda g, place: (0, 0)),
                pl.BlockSpec((rows, HEAD), col),
                pl.BlockSpec((rows, HEAD), col),
                pl.BlockSpec((prow, wide), pcol),
                pl.BlockSpec((prow, wide), pcol),
                pl.BlockSpec((1, 1, ratio * prow), plead),
                pl.BlockSpec((1, 1, ratio * prow), plead),
            ],
            out_specs=[
                pl.BlockSpec((n_pre, 1, 2, prow, HEAD), kv_at),
                pl.BlockSpec((rows, wide), col),
                pl.BlockSpec((rows, HEAD), col),
                pl.BlockSpec((rows, HEAD), col),
                pl.BlockSpec((prow, wide), pcol),
            ],
            scratch_shapes=[
                pltpu.VMEM((HEAD, ratio * rows), F32),
                pltpu.VMEM((HEAD, ratio * prow), F32),
            ],
        ),
        out_shape=[
            jax.ShapeDtypeStruct((n_pre, n_br, 2, prow, cols), F32),
            jax.ShapeDtypeStruct(resp_query.shape, BF16),
            jax.ShapeDtypeStruct(response_key_rows.shape, BF16),
            jax.ShapeDtypeStruct(response_value_rows.shape, BF16),
            jax.ShapeDtypeStruct(prompt_query.shape, BF16),
        ],
        compiler_params=pltpu.CompilerParams(vmem_limit_bytes=48 * 1024 * 1024),
        name="attention",
    )(
        place,
        kv_all,
        resp_query,
        resp_grad_out,
        rnorm,
        rdelta,
        bias,
        response_key_rows,
        response_value_rows,
        prompt_query,
        prompt_grad_out,
        pnorm,
        pdelta,
    )
    total = lax.psum_scatter(
        dkv.reshape(n_pre * n_br, 2, prow, cols), ("pre", "br"), scatter_dimension=0, tiled=False
    )
    return pdq, total[0].astype(BF16), total[1].astype(BF16), rdq, rdk, rdv


def solution(mesh):
    both = P("pre", "br")
    own = P(("pre", "br"), None)
    in_specs = (both,) * 6 + (own,) * 6 + (P(("pre", "br")),)
    out_specs = (both,) * 3 + (own,) * 3
    body = functools.partial(local, mesh.shape["pre"], mesh.shape["br"])
    return jax.shard_map(body, mesh=mesh, in_specs=in_specs, out_specs=out_specs, check_vma=False)
```

```python
import functools

import jax
import jax.numpy as jnp
from jax import lax
from jax.experimental import pallas as pl
from jax.experimental.pallas import tpu as pltpu
from jax.sharding import PartitionSpec as P

HEAD = 128
SCALE = HEAD ** (-0.5)
LOG2E = 1.4426950408889634
F32 = jnp.float32
BF16 = jnp.bfloat16


def dot(a, b, ca, cb):
    return lax.dot_general(a, b, (((ca,), (cb,)), ((), ())), preferred_element_type=F32)


def stack_heads(block):
    ratio = block.shape[1] // HEAD
    return jnp.concatenate([block[:, h * HEAD : (h + 1) * HEAD] for h in range(ratio)], 0)


def spread_heads(dq_t, rows):
    dq = dq_t.T
    ratio = dq.shape[0] // rows
    return jnp.concatenate([dq[h * rows : (h + 1) * rows] for h in range(ratio)], 1)


def terms(k, v, q, go, norm, delta, bias):
    s = dot(k, q, 1, 1)
    z = s * (SCALE * LOG2E) - norm
    if bias is not None:
        z = z + bias
    w = jnp.exp2(z)
    ds = w * (dot(v, go, 1, 1) - delta)
    wb = w.astype(BF16)
    dsb = ds.astype(BF16)
    return dot(dsb, q, 1, 0) * SCALE, dot(wb, go, 1, 0), dot(k, dsb, 0, 0)


def attention_kernel(
    chunk_blocks,
    place,
    kv_ref,
    rq_ref,
    rgo_ref,
    rnorm_ref,
    rdelta_ref,
    bias_ref,
    rk_ref,
    rv_ref,
    pq_ref,
    pgo_ref,
    pnorm_ref,
    pdelta_ref,
    dkv_ref,
    rdq_ref,
    rdk_ref,
    rdv_ref,
    pdq_ref,
    racc,
    pacc,
):
    n_pre, _, _, block_rows, _ = kv_ref.shape
    group = pl.program_id(0)
    pre = place[0]
    per_br = place[2]
    mine = (group // per_br) == place[1]
    rows = rq_ref.shape[0]
    prow = pq_ref.shape[0]
    chunk = chunk_blocks * block_rows
    rq = stack_heads(rq_ref[...])
    rgo = stack_heads(rgo_ref[...])
    rnorm = rnorm_ref[0]
    rdelta = rdelta_ref[0]
    dk, dv, dq = terms(rk_ref[...], rv_ref[...], rq, rgo, rnorm, rdelta, bias_ref[...])
    rdk_ref[...] = dk.astype(BF16)
    rdv_ref[...] = dv.astype(BF16)
    racc[...] = dq

    @pl.when(mine)
    def _():
        pacc[...] = jnp.zeros_like(pacc)

    for c in range(n_pre // chunk_blocks):
        at = pl.ds(c * chunk_blocks, chunk_blocks)
        k = kv_ref[at, 0, 0].reshape(chunk, HEAD)
        v = kv_ref[at, 0, 1].reshape(chunk, HEAD)
        dk, dv, dq = terms(k, v, rq, rgo, rnorm, rdelta, None)
        racc[...] += dq
        with_prompt = mine & (c * chunk < (pre + 1) * prow)

        @pl.when(with_prompt)
        def _():
            pq = stack_heads(pq_ref[...])
            pgo = stack_heads(pgo_ref[...])
            key = lax.broadcasted_iota(jnp.int32, (chunk, pq.shape[0]), 0) + c * chunk
            row = lax.rem(lax.broadcasted_iota(jnp.int32, (chunk, pq.shape[0]), 1), prow)
            bias = jnp.where(key <= row + pre * prow, 0.0, -1e30)
            pdk, pdv, pdq = terms(k, v, pq, pgo, pnorm_ref[0], pdelta_ref[0], bias)
            pacc[...] += pdq
            dkv_ref[at, 0, 0] = (dk + pdk).astype(BF16).reshape(chunk_blocks, block_rows, HEAD)
            dkv_ref[at, 0, 1] = (dv + pdv).astype(BF16).reshape(chunk_blocks, block_rows, HEAD)

        @pl.when(jnp.logical_not(with_prompt))
        def _():
            dkv_ref[at, 0, 0] = dk.astype(BF16).reshape(chunk_blocks, block_rows, HEAD)
            dkv_ref[at, 0, 1] = dv.astype(BF16).reshape(chunk_blocks, block_rows, HEAD)

    rdq_ref[...] = (spread_heads(racc[...], rows) * SCALE).astype(BF16)

    @pl.when(mine)
    def _():
        pdq_ref[...] = (spread_heads(pacc[...], prow) * SCALE).astype(BF16)


def position(nz, ny):
    pre = lax.axis_index("pre")
    y = lax.axis_index("br")
    z = pre // 4
    x = lax.rem(pre // 2, 2)
    c = lax.rem(pre, 2)
    index = lambda zz, xx, cc: (zz * 2 + xx) * 2 + cc
    around_z = [lax.rem(z + d, nz) for d in range(1, nz)]
    around_y = [lax.rem(y + d, ny) for d in range(1, ny)]
    return z, x, c, y, index, around_z, around_y


def greet(targets):
    barrier = pltpu.get_barrier_semaphore()
    for target in targets:
        pl.semaphore_signal(barrier, inc=1, device_id=target, device_id_type=pl.DeviceIdType.MESH)
    pl.semaphore_wait(barrier, len(targets))


def gather_kernel(nz, ny, own_ref, out_ref, send_sem, recv_sem, local_sem):
    z, x, c, y, index, around_z, around_y = position(nz, ny)
    sibling = (index(z, x, 1 - c), y)
    x_side = (index(z, 1 - x, c), y)
    y_side = [(index(z, x, c), yy) for yy in around_y]
    z_side = [(index(zz, x, c), y) for zz in around_z]
    greet([sibling, x_side] + y_side + z_side)
    sent = []

    def send(zz, xx, yy, t, target, mine=False):
        slot = index(zz, xx, c)
        copy = pltpu.make_async_remote_copy(
            src_ref=own_ref.at[t] if mine else out_ref.at[slot, yy, t],
            dst_ref=out_ref.at[slot, yy, t],
            send_sem=send_sem.at[len(sent)],
            recv_sem=recv_sem.at[slot, yy, t],
            device_id=target,
            device_id_type=pl.DeviceIdType.MESH,
        )
        copy.start()
        sent.append(copy)

    def arrive(zz, xx, yy, cc, t):
        at = out_ref.at[index(zz, xx, cc), yy, t]
        pltpu.make_async_copy(at, at, recv_sem.at[index(zz, xx, cc), yy, t]).wait()

    def column(zz, mine):
        for t in range(2):
            if not mine:
                arrive(zz, x, y, c, t)
            send(zz, x, y, t, x_side, mine)
            for target in y_side:
                send(zz, x, y, t, target, mine)
            send(zz, x, y, t, sibling, mine)

    def second(zz):
        for t in range(2):
            arrive(zz, 1 - x, y, c, t)
            if t == 0:
                for target in y_side:
                    send(zz, 1 - x, y, 0, target)
            send(zz, 1 - x, y, t, sibling)
            for yy in around_y:
                arrive(zz, x, yy, c, t)
                if t == 1:
                    send(zz, x, yy, 1, x_side)
                send(zz, x, yy, t, sibling)

    def third(zz):
        for t in range(2):
            for yy in around_y:
                arrive(zz, 1 - x, yy, c, t)
                send(zz, 1 - x, yy, t, sibling)

    for target in z_side:
        for t in range(2):
            send(z, x, y, t, target, True)
    keep = pltpu.make_async_copy(own_ref, out_ref.at[index(z, x, c), y], local_sem)
    keep.start()
    order = [z] + around_z
    for step in range(nz + 2):
        if step < nz:
            column(order[step], step == 0)
        if 0 <= step - 1 < nz:
            second(order[step - 1])
        if 0 <= step - 2 < nz:
            third(order[step - 2])
    for zz in order:
        for xx in range(2):
            for yy in [y] + around_y:
                for t in range(2):
                    arrive(zz, xx, yy, 1 - c, t)
    keep.wait()
    for copy in sent:
        copy.wait_send()


def gather(own, n_pre, n_br):
    nz = n_pre // 4
    copies = 2 * (nz - 1) + nz * (2 * (1 + n_br) + (n_br - 1) * 2 + 2 * n_br + 2 * (n_br - 1))
    return pl.pallas_call(
        functools.partial(gather_kernel, nz, n_br),
        out_shape=jax.ShapeDtypeStruct((n_pre, n_br) + own.shape, BF16),
        in_specs=[pl.BlockSpec(memory_space=pl.ANY)],
        out_specs=pl.BlockSpec(memory_space=pl.ANY),
        scratch_shapes=[
            pltpu.SemaphoreType.DMA((copies,)),
            pltpu.SemaphoreType.DMA((n_pre, n_br, 2)),
            pltpu.SemaphoreType.DMA,
        ],
        compiler_params=pltpu.CompilerParams(collective_id=0, has_side_effects=True),
        name="gather_keys",
    )(own)


def reduce_kernel(
    nz, ny, part_ref, out_ref, r0, rx, ry, ryk, rxv, sz, rz, send_sem, q0, qx, qy, qyk, qxv, qz
):
    z, x, c, y, index, around_z, around_y = position(nz, ny)
    sibling = (index(z, x, 1 - c), y)
    x_side = (index(z, 1 - x, c), y)
    y_side = [(index(z, x, c), yy) for yy in around_y]
    z_side = [(index(zz, x, c), y) for zz in around_z]
    greet([sibling, x_side] + y_side + z_side)
    order = around_z + [z]
    sent = []

    def send(src, dst, sem, target):
        copy = pltpu.make_async_remote_copy(
            src_ref=src,
            dst_ref=dst,
            send_sem=send_sem.at[len(sent)],
            recv_sem=sem,
            device_id=target,
            device_id_type=pl.DeviceIdType.MESH,
        )
        copy.start()
        sent.append(copy)

    def arrive(at, sem):
        pltpu.make_async_copy(at, at, sem).wait()

    for i, zz in enumerate(order):
        send(part_ref.at[zz, :, 1 - c], r0.at[i], q0.at[i], sibling)

    def first(i):
        arrive(r0.at[i], q0.at[i])
        for xx in range(2):
            for yy in range(ny):
                own = part_ref[order[i], xx, c, yy].astype(F32)
                r0[i, xx, yy] = (own + r0[i, xx, yy].astype(F32)).astype(BF16)
        send(r0.at[i, 1 - x, :, 0], rx.at[i], qx.at[i], x_side)
        for target, yy in zip(y_side, around_y):
            send(r0.at[i, :, yy, 1], ry.at[i, y], qy.at[i, y], target)

    def second(i):
        arrive(rx.at[i], qx.at[i])
        rx[i] = (r0[i, x, :, 0].astype(F32) + rx[i].astype(F32)).astype(BF16)
        for target, yy in zip(y_side, around_y):
            send(rx.at[i, yy], ryk.at[i, y], qyk.at[i, y], target)
        total = r0[i, :, y, 1].astype(F32)
        for yy in around_y:
            arrive(ry.at[i, yy], qy.at[i, yy])
            total = total + ry[i, yy].astype(F32)
        ry[i, y] = total.astype(BF16)
        send(ry.at[i, y, 1 - x], rxv.at[i], qxv.at[i], x_side)

    def third(i):
        total_k = rx[i, y].astype(F32)
        for yy in around_y:
            arrive(ryk.at[i, yy], qyk.at[i, yy])
            total_k = total_k + ryk[i, yy].astype(F32)
        arrive(rxv.at[i], qxv.at[i])
        total_v = ry[i, y, x].astype(F32) + rxv[i].astype(F32)
        if i < nz - 1:
            sz[i, 0] = total_k.astype(BF16)
            sz[i, 1] = total_v.astype(BF16)
            send(sz.at[i], rz.at[i], qz.at[i], z_side[i])
            return
        for j in range(nz - 1):
            arrive(rz.at[j], qz.at[j])
            total_k = total_k + rz[j, 0].astype(F32)
            total_v = total_v + rz[j, 1].astype(F32)
        out_ref[0] = total_k.astype(BF16)
        out_ref[1] = total_v.astype(BF16)

    for step in range(nz + 2):
        if step < nz:
            first(step)
        if 0 <= step - 1 < nz:
            second(step - 1)
        if 0 <= step - 2 < nz:
            third(step - 2)
    for copy in sent:
        copy.wait_send()


def reduce(part, n_pre, n_br):
    nz = n_pre // 4
    piece = part.shape[-2:]
    part = part.reshape((nz, 2, 2, n_br, 2) + piece)
    copies = nz + nz * (1 + (n_br - 1) + (n_br - 1) + 1) + nz - 1
    return pl.pallas_call(
        functools.partial(reduce_kernel, nz, n_br),
        out_shape=jax.ShapeDtypeStruct((2,) + piece, BF16),
        in_specs=[pl.BlockSpec(memory_space=pltpu.VMEM)],
        out_specs=pl.BlockSpec(memory_space=pltpu.VMEM),
        scratch_shapes=[
            pltpu.VMEM((nz, 2, n_br, 2) + piece, BF16),
            pltpu.VMEM((nz, n_br) + piece, BF16),
            pltpu.VMEM((nz, n_br, 2) + piece, BF16),
            pltpu.VMEM((nz, n_br) + piece, BF16),
            pltpu.VMEM((nz,) + piece, BF16),
            pltpu.VMEM((max(nz - 1, 1), 2) + piece, BF16),
            pltpu.VMEM((max(nz - 1, 1), 2) + piece, BF16),
            pltpu.SemaphoreType.DMA((copies,)),
            pltpu.SemaphoreType.DMA((nz,)),
            pltpu.SemaphoreType.DMA((nz,)),
            pltpu.SemaphoreType.DMA((nz, n_br)),
            pltpu.SemaphoreType.DMA((nz, n_br)),
            pltpu.SemaphoreType.DMA((nz,)),
            pltpu.SemaphoreType.DMA((max(nz - 1, 1),)),
        ],
        compiler_params=pltpu.CompilerParams(
            collective_id=1, has_side_effects=True, vmem_limit_bytes=48 * 1024 * 1024
        ),
        name="reduce_gradients",
    )(part)


def per_group(x, groups):
    rows, heads = x.shape
    return x.T.reshape(groups, 1, heads // groups * rows)


def local(
    n_pre,
    n_br,
    prompt_query,
    prompt_key_rows,
    prompt_value_rows,
    prompt_grad_out,
    prompt_lse,
    prompt_delta,
    resp_query,
    response_key_rows,
    response_value_rows,
    resp_grad_out,
    resp_lse,
    resp_delta,
    resp_segment,
):
    prow, cols = prompt_key_rows.shape
    rows, width = response_key_rows.shape
    groups = width // HEAD
    per_br = cols // HEAD
    ratio = resp_query.shape[1] // width
    wide = ratio * HEAD
    pre = lax.axis_index("pre").astype(jnp.int32)
    br = lax.axis_index("br").astype(jnp.int32)
    place = jnp.stack([pre, br, jnp.int32(per_br)])

    kv = jnp.stack([prompt_key_rows, prompt_value_rows])
    kv_all = gather(kv, n_pre, n_br)

    usable = (resp_segment >= 0)[:, None]
    rnorm = per_group(jnp.where(usable, resp_lse * LOG2E, 1e30), groups)
    rdelta = per_group(resp_delta, groups)
    pnorm = per_group(prompt_lse * LOG2E, per_br)
    pdelta = per_group(prompt_delta, per_br)
    index = jnp.arange(rows, dtype=jnp.int32)
    seen = (resp_segment[:, None] == resp_segment[None, :]) & (index[:, None] <= index[None, :])
    bias = jnp.tile(jnp.where(seen, 0.0, -1e30), (1, ratio))

    def kv_at(g, place):
        return (0, g // per_br, 0, 0, g % per_br)

    def prompt_g(g, place):
        return jnp.clip(g - place[1] * per_br, 0, per_br - 1)

    chunk_blocks = max(1, 256 // prow)
    col = lambda g, place: (0, g)
    pcol = lambda g, place: (0, prompt_g(g, place))
    lead = lambda g, place: (g, 0, 0)
    plead = lambda g, place: (prompt_g(g, place), 0, 0)
    dkv, rdq, rdk, rdv, pdq = pl.pallas_call(
        functools.partial(attention_kernel, chunk_blocks),
        grid_spec=pltpu.PrefetchScalarGridSpec(
            num_scalar_prefetch=1,
            grid=(groups,),
            in_specs=[
                pl.BlockSpec((n_pre, 1, 2, prow, HEAD), kv_at),
                pl.BlockSpec((rows, wide), col),
                pl.BlockSpec((rows, wide), col),
                pl.BlockSpec((1, 1, ratio * rows), lead),
                pl.BlockSpec((1, 1, ratio * rows), lead),
                pl.BlockSpec((rows, ratio * rows), lambda g, place: (0, 0)),
                pl.BlockSpec((rows, HEAD), col),
                pl.BlockSpec((rows, HEAD), col),
                pl.BlockSpec((prow, wide), pcol),
                pl.BlockSpec((prow, wide), pcol),
                pl.BlockSpec((1, 1, ratio * prow), plead),
                pl.BlockSpec((1, 1, ratio * prow), plead),
            ],
            out_specs=[
                pl.BlockSpec((n_pre, 1, 2, prow, HEAD), kv_at),
                pl.BlockSpec((rows, wide), col),
                pl.BlockSpec((rows, HEAD), col),
                pl.BlockSpec((rows, HEAD), col),
                pl.BlockSpec((prow, wide), pcol),
            ],
            scratch_shapes=[
                pltpu.VMEM((HEAD, ratio * rows), F32),
                pltpu.VMEM((HEAD, ratio * prow), F32),
            ],
        ),
        out_shape=[
            jax.ShapeDtypeStruct((n_pre, n_br, 2, prow, cols), BF16),
            jax.ShapeDtypeStruct(resp_query.shape, BF16),
            jax.ShapeDtypeStruct(response_key_rows.shape, BF16),
            jax.ShapeDtypeStruct(response_value_rows.shape, BF16),
            jax.ShapeDtypeStruct(prompt_query.shape, BF16),
        ],
        compiler_params=pltpu.CompilerParams(vmem_limit_bytes=48 * 1024 * 1024),
        name="attention",
    )(
        place,
        kv_all,
        resp_query,
        resp_grad_out,
        rnorm,
        rdelta,
        bias,
        response_key_rows,
        response_value_rows,
        prompt_query,
        prompt_grad_out,
        pnorm,
        pdelta,
    )
    total = reduce(dkv, n_pre, n_br)
    return pdq, total[0], total[1], rdq, rdk, rdv


def solution(mesh):
    both = P("pre", "br")
    own = P(("pre", "br"), None)
    in_specs = (both,) * 6 + (own,) * 6 + (P(("pre", "br")),)
    out_specs = (both,) * 3 + (own,) * 3
    body = functools.partial(local, mesh.shape["pre"], mesh.shape["br"])
    return jax.shard_map(body, mesh=mesh, in_specs=in_specs, out_specs=out_specs, check_vma=False)
```

```python
import functools

import jax
import jax.numpy as jnp
from jax import lax
from jax.experimental import pallas as pl
from jax.experimental.pallas import tpu as pltpu
from jax.sharding import PartitionSpec as P

HEAD = 128
SCALE = HEAD ** (-0.5)
LOG2E = 1.4426950408889634
F32 = jnp.float32
BF16 = jnp.bfloat16


def dot(a, b, ca, cb):
    return lax.dot_general(a, b, (((ca,), (cb,)), ((), ())), preferred_element_type=F32)


def stack_heads(block):
    ratio = block.shape[1] // HEAD
    return jnp.concatenate([block[:, h * HEAD : (h + 1) * HEAD] for h in range(ratio)], 0)


def spread_heads(dq_t, rows):
    dq = dq_t.T
    ratio = dq.shape[0] // rows
    return jnp.concatenate([dq[h * rows : (h + 1) * rows] for h in range(ratio)], 1)


def terms(k, v, q, go, norm, delta, bias):
    s = dot(k, q, 1, 1)
    z = s * (SCALE * LOG2E) - norm
    if bias is not None:
        z = z + bias
    w = jnp.exp2(z)
    ds = w * (dot(v, go, 1, 1) - delta)
    wb = w.astype(BF16)
    dsb = ds.astype(BF16)
    return dot(dsb, q, 1, 0) * SCALE, dot(wb, go, 1, 0), dot(k, dsb, 0, 0)


def position(nz, ny):
    pre = lax.axis_index("pre")
    y = lax.axis_index("br")
    z = pre // 4
    x = lax.rem(pre // 2, 2)
    c = lax.rem(pre, 2)
    index = lambda zz, xx, cc: (zz * 2 + xx) * 2 + cc
    around_z = [lax.rem(z + d, nz) for d in range(1, nz)]
    around_y = [lax.rem(y + d, ny) for d in range(1, ny)]
    return z, x, c, y, index, around_z, around_y


def greet(targets):
    barrier = pltpu.get_barrier_semaphore()
    for target in targets:
        pl.semaphore_signal(barrier, inc=1, device_id=target, device_id_type=pl.DeviceIdType.MESH)
    pl.semaphore_wait(barrier, len(targets))


def fused_kernel(
    nz,
    ny,
    own_ref,
    rq_ref,
    rgo_ref,
    rnorm_ref,
    rdelta_ref,
    bias_ref,
    rk_ref,
    rv_ref,
    pq_ref,
    pgo_ref,
    pnorm_ref,
    pdelta_ref,
    out_ref,
    rdq_ref,
    rdk_ref,
    rdv_ref,
    pdq_ref,
    kv,
    part,
    racc,
    pacc,
    r0,
    rx,
    ry,
    ryk,
    rxv,
    sz,
    rz,
    fin,
    send_sem,
    recv_sem,
    local_sem,
    q0,
    qx,
    qy,
    qyk,
    qxv,
    qz,
):
    z, x, c, y, index, around_z, around_y = position(nz, ny)
    sibling = (index(z, x, 1 - c), y)
    x_side = (index(z, 1 - x, c), y)
    y_side = [(index(z, x, c), yy) for yy in around_y]
    z_side = [(index(zz, x, c), y) for zz in around_z]
    greet([sibling, x_side] + y_side + z_side)
    order = [z] + around_z
    sent = []
    rows = rk_ref.shape[0]
    groups = rk_ref.shape[1] // HEAD
    _, prow, cols = own_ref.shape
    per_br = cols // HEAD
    wide = rq_ref.shape[1] // groups
    chunk = 4 * prow

    def push(src, dst, sem, target):
        copy = pltpu.make_async_remote_copy(
            src_ref=src,
            dst_ref=dst,
            send_sem=send_sem.at[len(sent)],
            recv_sem=sem,
            device_id=target,
            device_id_type=pl.DeviceIdType.MESH,
        )
        copy.start()
        sent.append(copy)

    def landed(at, sem):
        pltpu.make_async_copy(at, at, sem).wait()

    def send(zz, xx, yy, t, target, mine=False):
        slot = index(zz, xx, c)
        src = own_ref.at[t] if mine else kv.at[slot, yy, t]
        push(src, kv.at[slot, yy, t], recv_sem.at[slot, yy, t], target)

    def arrive(zz, xx, yy, cc, t):
        slot = index(zz, xx, cc)
        landed(kv.at[slot, yy, t], recv_sem.at[slot, yy, t])

    def column(i):
        zz = order[i]
        for t in range(2):
            if i > 0:
                arrive(zz, x, y, c, t)
            send(zz, x, y, t, x_side, i == 0)
            for target in y_side:
                send(zz, x, y, t, target, i == 0)
            send(zz, x, y, t, sibling, i == 0)

    def second(i):
        zz = order[i]
        for t in range(2):
            arrive(zz, 1 - x, y, c, t)
            if t == 0:
                for target in y_side:
                    send(zz, 1 - x, y, 0, target)
            send(zz, 1 - x, y, t, sibling)
            for yy in around_y:
                arrive(zz, x, yy, c, t)
                if t == 1:
                    send(zz, x, yy, 1, x_side)
                send(zz, x, yy, t, sibling)

    def third(i):
        zz = order[i]
        for t in range(2):
            for yy in around_y:
                arrive(zz, 1 - x, yy, c, t)
                send(zz, 1 - x, yy, t, sibling)

    def from_sibling(i):
        for xx in range(2):
            for yy in [y] + around_y:
                for t in range(2):
                    arrive(order[i], xx, yy, 1 - c, t)

    def cut(ref, g, width):
        return ref[:, pl.ds(pl.multiple_of(g * width, width), width)]

    def near(g, carry):
        at = pl.ds(pl.multiple_of(g * HEAD, HEAD), HEAD)
        rq = stack_heads(cut(rq_ref, g, wide))
        rgo = stack_heads(cut(rgo_ref, g, wide))
        dk, dv, dq = terms(
            rk_ref[:, at], rv_ref[:, at], rq, rgo, rnorm_ref[g], rdelta_ref[g], bias_ref[...]
        )
        rdk_ref[:, at] = dk.astype(BF16)
        rdv_ref[:, at] = dv.astype(BF16)
        racc[g] = dq
        return carry

    def far(i, g, carry):
        zz = order[i]
        owner = g // per_br
        lane = pl.ds(pl.multiple_of(lax.rem(g, per_br) * HEAD, HEAD), HEAD)
        k = kv[pl.ds(zz * 4, 4), owner, 0, :, lane].reshape(chunk, HEAD)
        v = kv[pl.ds(zz * 4, 4), owner, 1, :, lane].reshape(chunk, HEAD)
        rq = stack_heads(cut(rq_ref, g, wide))
        rgo = stack_heads(cut(rgo_ref, g, wide))
        dk, dv, dq = terms(k, v, rq, rgo, rnorm_ref[g], rdelta_ref[g], None)
        racc[g] += dq

        def put(dk, dv):
            for xx in range(2):
                for cc in range(2):
                    first_row = (xx * 2 + cc) * prow
                    piece = slice(first_row, first_row + prow)
                    part[zz, xx, cc, owner, 0, :, lane] = dk[piece].astype(BF16)
                    part[zz, xx, cc, owner, 1, :, lane] = dv[piece].astype(BF16)

        with_prompt = (owner == y) & (zz <= z)

        @pl.when(with_prompt)
        def _():
            own = g - y * per_br
            pq = stack_heads(cut(pq_ref, own, wide))
            pgo = stack_heads(cut(pgo_ref, own, wide))
            bias = None
            if i == 0:
                key = lax.broadcasted_iota(jnp.int32, (chunk, pq.shape[0]), 0)
                row = lax.rem(lax.broadcasted_iota(jnp.int32, (chunk, pq.shape[0]), 1), prow)
                bias = jnp.where(key <= row + (x * 2 + c) * prow, 0.0, -1e30)
            pdk, pdv, pdq = terms(k, v, pq, pgo, pnorm_ref[own], pdelta_ref[own], bias)
            if i == 0:
                pacc[own] = pdq
            else:
                pacc[own] += pdq
            put(dk + pdk, dv + pdv)

        @pl.when(jnp.logical_not(with_prompt))
        def _():
            put(dk, dv)

        return carry

    def compute(i, half):
        low, high = (0, groups // 2) if half == 0 else (groups // 2, groups)
        lax.fori_loop(low, high, functools.partial(far, i), 0)

    def swap(i):
        push(part.at[order[i], :, 1 - c], r0.at[i], q0.at[i], sibling)

    def reduce_first(i):
        landed(r0.at[i], q0.at[i])
        for xx in range(2):
            for yy in range(ny):
                own = part[order[i], xx, c, yy].astype(F32)
                r0[i, xx, yy] = (own + r0[i, xx, yy].astype(F32)).astype(BF16)
        push(r0.at[i, 1 - x, :, 0], rx.at[i], qx.at[i], x_side)
        for target, yy in zip(y_side, around_y):
            push(r0.at[i, :, yy, 1], ry.at[i, y], qy.at[i, y], target)

    def reduce_second(i):
        landed(rx.at[i], qx.at[i])
        rx[i] = (r0[i, x, :, 0].astype(F32) + rx[i].astype(F32)).astype(BF16)
        for target, yy in zip(y_side, around_y):
            push(rx.at[i, yy], ryk.at[i, y], qyk.at[i, y], target)
        total = r0[i, :, y, 1].astype(F32)
        for yy in around_y:
            landed(ry.at[i, yy], qy.at[i, yy])
            total = total + ry[i, yy].astype(F32)
        ry[i, y] = total.astype(BF16)
        push(ry.at[i, y, 1 - x], rxv.at[i], qxv.at[i], x_side)

    def reduce_third(i):
        total_k = rx[i, y].astype(F32)
        for yy in around_y:
            landed(ryk.at[i, yy], qyk.at[i, yy])
            total_k = total_k + ryk[i, yy].astype(F32)
        landed(rxv.at[i], qxv.at[i])
        total_v = ry[i, y, x].astype(F32) + rxv[i].astype(F32)
        if i == 0:
            fin[0] = total_k
            fin[1] = total_v
        else:
            sz[i - 1, 0] = total_k.astype(BF16)
            sz[i - 1, 1] = total_v.astype(BF16)
            push(sz.at[i - 1], rz.at[i - 1], qz.at[i - 1], z_side[i - 1])

    for target in z_side:
        for t in range(2):
            send(z, x, y, t, target, True)
    keep = pltpu.make_async_copy(own_ref, kv.at[index(z, x, c), y], local_sem)
    keep.start()
    column(0)
    lax.fori_loop(0, groups, near, 0)
    second(0)
    if nz > 1:
        column(1)
    third(0)
    keep.wait()
    for i in range(nz):
        from_sibling(i)
        compute(i, 0)
        if i + 1 < nz:
            second(i + 1)
        if i + 2 < nz:
            column(i + 2)
        if i >= 1:
            reduce_first(i - 1)
        compute(i, 1)
        swap(i)
        if i + 1 < nz:
            third(i + 1)
        if i >= 1:
            reduce_second(i - 1)
        if i >= 2:
            reduce_third(i - 2)

    def finish(g, carry):
        at = pl.ds(pl.multiple_of(g * wide, wide), wide)
        rdq_ref[:, at] = (spread_heads(racc[g], rows) * SCALE).astype(BF16)
        return carry

    def finish_prompt(g, carry):
        at = pl.ds(pl.multiple_of(g * wide, wide), wide)
        pdq_ref[:, at] = (spread_heads(pacc[g], prow) * SCALE).astype(BF16)
        return carry

    lax.fori_loop(0, per_br, finish_prompt, 0)
    reduce_first(nz - 1)
    if nz > 1:
        reduce_third(nz - 2)
    lax.fori_loop(0, groups, finish, 0)
    reduce_second(nz - 1)
    reduce_third(nz - 1)
    total = fin[...]
    for j in range(nz - 1):
        landed(rz.at[j], qz.at[j])
        total = total + rz[j].astype(F32)
    out_ref[...] = total.astype(BF16)
    for copy in sent:
        copy.wait_send()


def per_group(x, groups):
    rows, heads = x.shape
    return x.T.reshape(groups, 1, heads // groups * rows)


def local(
    n_pre,
    n_br,
    prompt_query,
    prompt_key_rows,
    prompt_value_rows,
    prompt_grad_out,
    prompt_lse,
    prompt_delta,
    resp_query,
    response_key_rows,
    response_value_rows,
    resp_grad_out,
    resp_lse,
    resp_delta,
    resp_segment,
):
    prow, cols = prompt_key_rows.shape
    rows, width = response_key_rows.shape
    groups = width // HEAD
    per_br = cols // HEAD
    ratio = resp_query.shape[1] // width
    kv = jnp.stack([prompt_key_rows, prompt_value_rows])
    usable = (resp_segment >= 0)[:, None]
    rnorm = per_group(jnp.where(usable, resp_lse * LOG2E, 1e30), groups)
    rdelta = per_group(resp_delta, groups)
    pnorm = per_group(prompt_lse * LOG2E, per_br)
    pdelta = per_group(prompt_delta, per_br)
    index = jnp.arange(rows, dtype=jnp.int32)
    seen = (resp_segment[:, None] == resp_segment[None, :]) & (index[:, None] <= index[None, :])
    bias = jnp.tile(jnp.where(seen, 0.0, -1e30), (1, ratio))

    nz = n_pre // 4
    piece = (prow, cols)
    copies = 2 * (nz - 1) + nz * (2 * (1 + n_br) + (n_br - 1) * 2 + 2 * n_br + 2 * (n_br - 1))
    copies += nz + nz * (1 + (n_br - 1) + (n_br - 1) + 1) + nz - 1
    others = max(nz - 1, 1)
    sem = pltpu.SemaphoreType.DMA
    vmem = pl.BlockSpec(memory_space=pltpu.VMEM)
    total, rdq, rdk, rdv, pdq = pl.pallas_call(
        functools.partial(fused_kernel, nz, n_br),
        in_specs=[vmem] * 12,
        out_specs=[vmem] * 5,
        out_shape=[
            jax.ShapeDtypeStruct((2,) + piece, BF16),
            jax.ShapeDtypeStruct(resp_query.shape, BF16),
            jax.ShapeDtypeStruct(response_key_rows.shape, BF16),
            jax.ShapeDtypeStruct(response_value_rows.shape, BF16),
            jax.ShapeDtypeStruct(prompt_query.shape, BF16),
        ],
        scratch_shapes=[
            pltpu.VMEM((n_pre, n_br, 2) + piece, BF16),
            pltpu.VMEM((nz, 2, 2, n_br, 2) + piece, BF16),
            pltpu.VMEM((groups, HEAD, ratio * rows), F32),
            pltpu.VMEM((per_br, HEAD, ratio * prow), F32),
            pltpu.VMEM((nz, 2, n_br, 2) + piece, BF16),
            pltpu.VMEM((nz, n_br) + piece, BF16),
            pltpu.VMEM((nz, n_br, 2) + piece, BF16),
            pltpu.VMEM((nz, n_br) + piece, BF16),
            pltpu.VMEM((nz,) + piece, BF16),
            pltpu.VMEM((others, 2) + piece, BF16),
            pltpu.VMEM((others, 2) + piece, BF16),
            pltpu.VMEM((2,) + piece, F32),
            sem((copies,)),
            sem((n_pre, n_br, 2)),
            sem,
            sem((nz,)),
            sem((nz,)),
            sem((nz, n_br)),
            sem((nz, n_br)),
            sem((nz,)),
            sem((others,)),
        ],
        compiler_params=pltpu.CompilerParams(
            collective_id=0, has_side_effects=True, vmem_limit_bytes=52 * 1024 * 1024
        ),
        name="attention_backward",
    )(
        kv,
        resp_query,
        resp_grad_out,
        rnorm,
        rdelta,
        bias,
        response_key_rows,
        response_value_rows,
        prompt_query,
        prompt_grad_out,
        pnorm,
        pdelta,
    )
    return pdq, total[0], total[1], rdq, rdk, rdv


def solution(mesh):
    both = P("pre", "br")
    own = P(("pre", "br"), None)
    in_specs = (both,) * 6 + (own,) * 6 + (P(("pre", "br")),)
    out_specs = (both,) * 3 + (own,) * 3
    body = functools.partial(local, mesh.shape["pre"], mesh.shape["br"])
    return jax.shard_map(body, mesh=mesh, in_specs=in_specs, out_specs=out_specs, check_vma=False)
```

```python
import functools

import jax
import jax.numpy as jnp
from jax import lax
from jax.experimental import pallas as pl
from jax.experimental.pallas import tpu as pltpu
from jax.sharding import PartitionSpec as P

HEAD = 128
SCALE = HEAD ** (-0.5)
LOG2E = 1.4426950408889634
F32 = jnp.float32
BF16 = jnp.bfloat16


def dot(a, b, ca, cb):
    return lax.dot_general(a, b, (((ca,), (cb,)), ((), ())), preferred_element_type=F32)


def stack_heads(block):
    ratio = block.shape[1] // HEAD
    return jnp.concatenate([block[:, h * HEAD : (h + 1) * HEAD] for h in range(ratio)], 0)


def spread_heads(dq_t, rows):
    dq = dq_t.T
    ratio = dq.shape[0] // rows
    return jnp.concatenate([dq[h * rows : (h + 1) * rows] for h in range(ratio)], 1)


def terms(k, v, q, go, norm, delta, bias):
    s = dot(k, q, 1, 1)
    z = s * (SCALE * LOG2E) - norm
    if bias is not None:
        z = z + bias
    w = jnp.exp2(z)
    ds = w * (dot(v, go, 1, 1) - delta)
    wb = w.astype(BF16)
    dsb = ds.astype(BF16)
    return dot(dsb, q, 1, 0) * SCALE, dot(wb, go, 1, 0), dot(k, dsb, 0, 0)


def position(nz, ny):
    pre = lax.axis_index("pre")
    y = lax.axis_index("br")
    z = pre // 4
    x = lax.rem(pre // 2, 2)
    c = lax.rem(pre, 2)
    index = lambda zz, xx, cc: (zz * 2 + xx) * 2 + cc
    around_z = [lax.rem(z + d, nz) for d in range(1, nz)]
    around_y = [lax.rem(y + d, ny) for d in range(1, ny)]
    return z, x, c, y, index, around_z, around_y


def greet(targets):
    barrier = pltpu.get_barrier_semaphore()
    for target in targets:
        pl.semaphore_signal(barrier, inc=1, device_id=target, device_id_type=pl.DeviceIdType.MESH)
    pl.semaphore_wait(barrier, len(targets))


def fused_kernel(
    nz,
    ny,
    own_ref,
    rq_ref,
    rgo_ref,
    rnorm_ref,
    rdelta_ref,
    bias_ref,
    rk_ref,
    rv_ref,
    pq_ref,
    pgo_ref,
    pnorm_ref,
    pdelta_ref,
    pdk_ref,
    pdv_ref,
    rdq_ref,
    rdk_ref,
    rdv_ref,
    pdq_ref,
    kv,
    part,
    racc,
    pacc,
    r0,
    rx,
    ry,
    ryk,
    rxv,
    sz,
    rz,
    fin,
    send_sem,
    recv_sem,
    local_sem,
    q0,
    qx,
    qy,
    qyk,
    qxv,
    qz,
):
    z, x, c, y, index, around_z, around_y = position(nz, ny)
    sibling = (index(z, x, 1 - c), y)
    x_side = (index(z, 1 - x, c), y)
    y_side = [(index(z, x, c), yy) for yy in around_y]
    z_side = [(index(zz, x, c), y) for zz in around_z]
    greet([sibling, x_side] + y_side + z_side)
    order = [z] + around_z
    sent = []
    rows = rk_ref.shape[0]
    groups = rk_ref.shape[1] // HEAD
    _, prow, cols = own_ref.shape
    per_br = cols // HEAD
    wide = rq_ref.shape[1] // groups
    chunk = 4 * prow

    def push(src, dst, sem, target):
        copy = pltpu.make_async_remote_copy(
            src_ref=src,
            dst_ref=dst,
            send_sem=send_sem.at[len(sent)],
            recv_sem=sem,
            device_id=target,
            device_id_type=pl.DeviceIdType.MESH,
        )
        copy.start()
        sent.append(copy)

    def landed(at, sem):
        pltpu.make_async_copy(at, at, sem).wait()

    def send(zz, xx, yy, t, target, mine=False):
        slot = index(zz, xx, c)
        src = own_ref.at[t] if mine else kv.at[slot, yy, t]
        push(src, kv.at[slot, yy, t], recv_sem.at[slot, yy, t], target)

    def arrive(zz, xx, yy, cc, t):
        slot = index(zz, xx, cc)
        landed(kv.at[slot, yy, t], recv_sem.at[slot, yy, t])

    def column(i):
        zz = order[i]
        for t in range(2):
            if i > 0:
                arrive(zz, x, y, c, t)
            send(zz, x, y, t, x_side, i == 0)
            for target in y_side:
                send(zz, x, y, t, target, i == 0)
            send(zz, x, y, t, sibling, i == 0)

    def second(i):
        zz = order[i]
        for t in range(2):
            arrive(zz, 1 - x, y, c, t)
            if t == 0:
                for target in y_side:
                    send(zz, 1 - x, y, 0, target)
            send(zz, 1 - x, y, t, sibling)
            for yy in around_y:
                arrive(zz, x, yy, c, t)
                if t == 1:
                    send(zz, x, yy, 1, x_side)
                send(zz, x, yy, t, sibling)

    def third(i):
        zz = order[i]
        for t in range(2):
            for yy in around_y:
                arrive(zz, 1 - x, yy, c, t)
                send(zz, 1 - x, yy, t, sibling)

    def from_sibling(i):
        for xx in range(2):
            for yy in [y] + around_y:
                for t in range(2):
                    arrive(order[i], xx, yy, 1 - c, t)

    def cut(ref, g, width):
        return ref[:, pl.ds(pl.multiple_of(g * width, width), width)]

    def near(g, carry):
        at = pl.ds(pl.multiple_of(g * HEAD, HEAD), HEAD)
        rq = stack_heads(cut(rq_ref, g, wide))
        rgo = stack_heads(cut(rgo_ref, g, wide))
        dk, dv, dq = terms(
            rk_ref[:, at], rv_ref[:, at], rq, rgo, rnorm_ref[g], rdelta_ref[g], bias_ref[...]
        )
        rdk_ref[:, at] = dk.astype(BF16)
        rdv_ref[:, at] = dv.astype(BF16)
        racc[g] = dq
        return carry

    def far(i, g, carry):
        zz = order[i]
        owner = g // per_br
        lane = pl.ds(pl.multiple_of(lax.rem(g, per_br) * HEAD, HEAD), HEAD)
        k = kv[pl.ds(zz * 4, 4), owner, 0, :, lane].reshape(chunk, HEAD)
        v = kv[pl.ds(zz * 4, 4), owner, 1, :, lane].reshape(chunk, HEAD)
        rq = stack_heads(cut(rq_ref, g, wide))
        rgo = stack_heads(cut(rgo_ref, g, wide))
        dk, dv, dq = terms(k, v, rq, rgo, rnorm_ref[g], rdelta_ref[g], None)
        racc[g] += dq

        def put(dk, dv):
            for xx in range(2):
                for cc in range(2):
                    first_row = (xx * 2 + cc) * prow
                    piece = slice(first_row, first_row + prow)
                    part[zz, xx, cc, owner, 0, :, lane] = dk[piece].astype(BF16)
                    part[zz, xx, cc, owner, 1, :, lane] = dv[piece].astype(BF16)

        with_prompt = (owner == y) & (zz <= z)

        @pl.when(with_prompt)
        def _():
            own = g - y * per_br
            pq = stack_heads(cut(pq_ref, own, wide))
            pgo = stack_heads(cut(pgo_ref, own, wide))
            bias = None
            if i == 0:
                key = lax.broadcasted_iota(jnp.int32, (chunk, pq.shape[0]), 0)
                row = lax.rem(lax.broadcasted_iota(jnp.int32, (chunk, pq.shape[0]), 1), prow)
                bias = jnp.where(key <= row + (x * 2 + c) * prow, 0.0, -1e30)
            pdk, pdv, pdq = terms(k, v, pq, pgo, pnorm_ref[own], pdelta_ref[own], bias)
            if i == 0:
                pacc[own] = pdq
            else:
                pacc[own] += pdq
            put(dk + pdk, dv + pdv)

        @pl.when(jnp.logical_not(with_prompt))
        def _():
            put(dk, dv)

        return carry

    def compute(i, half):
        low, high = (0, groups // 2) if half == 0 else (groups // 2, groups)
        lax.fori_loop(low, high, functools.partial(far, i), 0)

    halves = 2 if ny % 2 == 0 else 1

    def owners(half):
        return pl.ds(half * (ny // halves), ny // halves)

    def swap(i, half):
        at = owners(half)
        push(part.at[order[i], :, 1 - c, at], r0.at[i, :, at], q0.at[i, half], sibling)

    def reduce_first(i):
        for half in range(halves):
            landed(r0.at[i, :, owners(half)], q0.at[i, half])
        for xx in range(2):
            for yy in range(ny):
                own = part[order[i], xx, c, yy].astype(F32)
                r0[i, xx, yy] = (own + r0[i, xx, yy].astype(F32)).astype(BF16)
        push(r0.at[i, 1 - x, :, 0], rx.at[i], qx.at[i], x_side)
        for target, yy in zip(y_side, around_y):
            push(r0.at[i, :, yy, 1], ry.at[i, y], qy.at[i, y], target)

    def reduce_second(i):
        landed(rx.at[i], qx.at[i])
        rx[i] = (r0[i, x, :, 0].astype(F32) + rx[i].astype(F32)).astype(BF16)
        for target, yy in zip(y_side, around_y):
            push(rx.at[i, yy], ryk.at[i, y], qyk.at[i, y], target)
        total = r0[i, :, y, 1].astype(F32)
        for yy in around_y:
            landed(ry.at[i, yy], qy.at[i, yy])
            total = total + ry[i, yy].astype(F32)
        ry[i, y] = total.astype(BF16)
        push(ry.at[i, y, 1 - x], rxv.at[i], qxv.at[i], x_side)

    def reduce_third(i):
        total_k = rx[i, y].astype(F32)
        for yy in around_y:
            landed(ryk.at[i, yy], qyk.at[i, yy])
            total_k = total_k + ryk[i, yy].astype(F32)
        landed(rxv.at[i], qxv.at[i])
        total_v = ry[i, y, x].astype(F32) + rxv[i].astype(F32)
        if i == 0:
            fin[0] = total_k
            fin[1] = total_v
        else:
            sz[i - 1, 0] = total_k.astype(BF16)
            sz[i - 1, 1] = total_v.astype(BF16)
            push(sz.at[i - 1], rz.at[i - 1], qz.at[i - 1], z_side[i - 1])

    for target in z_side:
        for t in range(2):
            send(z, x, y, t, target, True)
    keep = pltpu.make_async_copy(own_ref, kv.at[index(z, x, c), y], local_sem)
    keep.start()
    column(0)
    lax.fori_loop(0, groups, near, 0)
    second(0)
    if nz > 1:
        column(1)
    third(0)
    keep.wait()
    for i in range(nz):
        from_sibling(i)
        compute(i, 0)
        if halves == 2:
            swap(i, 0)
        if i + 1 < nz:
            second(i + 1)
        if i + 2 < nz:
            column(i + 2)
        if i >= 1:
            reduce_first(i - 1)
        compute(i, 1)
        swap(i, halves - 1)
        if i + 1 < nz:
            third(i + 1)
        if i >= 1:
            reduce_second(i - 1)
        if i >= 2:
            reduce_third(i - 2)

    def finish(g, carry):
        at = pl.ds(pl.multiple_of(g * wide, wide), wide)
        rdq_ref[:, at] = (spread_heads(racc[g], rows) * SCALE).astype(BF16)
        return carry

    def finish_prompt(g, carry):
        at = pl.ds(pl.multiple_of(g * wide, wide), wide)
        pdq_ref[:, at] = (spread_heads(pacc[g], prow) * SCALE).astype(BF16)
        return carry

    lax.fori_loop(0, per_br, finish_prompt, 0)
    reduce_first(nz - 1)
    if nz > 1:
        reduce_third(nz - 2)
    lax.fori_loop(0, groups, finish, 0)
    reduce_second(nz - 1)
    reduce_third(nz - 1)
    total = fin[...]
    for j in range(nz - 1):
        landed(rz.at[j], qz.at[j])
        total = total + rz[j].astype(F32)
    pdk_ref[...] = total[0].astype(BF16)
    pdv_ref[...] = total[1].astype(BF16)
    for copy in sent:
        copy.wait_send()


def per_group(x, groups):
    rows, heads = x.shape
    return x.T.reshape(groups, 1, heads // groups * rows)


def local(
    n_pre,
    n_br,
    prompt_query,
    prompt_key_rows,
    prompt_value_rows,
    prompt_grad_out,
    prompt_lse,
    prompt_delta,
    resp_query,
    response_key_rows,
    response_value_rows,
    resp_grad_out,
    resp_lse,
    resp_delta,
    resp_segment,
):
    prow, cols = prompt_key_rows.shape
    rows, width = response_key_rows.shape
    groups = width // HEAD
    per_br = cols // HEAD
    ratio = resp_query.shape[1] // width
    kv = jnp.stack([prompt_key_rows, prompt_value_rows])
    usable = (resp_segment >= 0)[:, None]
    rnorm = per_group(jnp.where(usable, resp_lse * LOG2E, 1e30), groups)
    rdelta = per_group(resp_delta, groups)
    pnorm = per_group(prompt_lse * LOG2E, per_br)
    pdelta = per_group(prompt_delta, per_br)
    index = jnp.arange(rows, dtype=jnp.int32)
    seen = (resp_segment[:, None] == resp_segment[None, :]) & (index[:, None] <= index[None, :])
    bias = jnp.tile(jnp.where(seen, 0.0, -1e30), (1, ratio))

    nz = n_pre // 4
    piece = (prow, cols)
    copies = 2 * (nz - 1) + nz * (2 * (1 + n_br) + (n_br - 1) * 2 + 2 * n_br + 2 * (n_br - 1))
    copies += 2 * nz + nz * (1 + (n_br - 1) + (n_br - 1) + 1) + nz - 1
    others = max(nz - 1, 1)
    sem = pltpu.SemaphoreType.DMA
    vmem = pl.BlockSpec(memory_space=pltpu.VMEM)
    pdk, pdv, rdq, rdk, rdv, pdq = pl.pallas_call(
        functools.partial(fused_kernel, nz, n_br),
        in_specs=[vmem] * 12,
        out_specs=[vmem] * 6,
        out_shape=[
            jax.ShapeDtypeStruct(piece, BF16),
            jax.ShapeDtypeStruct(piece, BF16),
            jax.ShapeDtypeStruct(resp_query.shape, BF16),
            jax.ShapeDtypeStruct(response_key_rows.shape, BF16),
            jax.ShapeDtypeStruct(response_value_rows.shape, BF16),
            jax.ShapeDtypeStruct(prompt_query.shape, BF16),
        ],
        scratch_shapes=[
            pltpu.VMEM((n_pre, n_br, 2) + piece, BF16),
            pltpu.VMEM((nz, 2, 2, n_br, 2) + piece, BF16),
            pltpu.VMEM((groups, HEAD, ratio * rows), F32),
            pltpu.VMEM((per_br, HEAD, ratio * prow), F32),
            pltpu.VMEM((nz, 2, n_br, 2) + piece, BF16),
            pltpu.VMEM((nz, n_br) + piece, BF16),
            pltpu.VMEM((nz, n_br, 2) + piece, BF16),
            pltpu.VMEM((nz, n_br) + piece, BF16),
            pltpu.VMEM((nz,) + piece, BF16),
            pltpu.VMEM((others, 2) + piece, BF16),
            pltpu.VMEM((others, 2) + piece, BF16),
            pltpu.VMEM((2,) + piece, F32),
            sem((copies,)),
            sem((n_pre, n_br, 2)),
            sem,
            sem((nz, 2)),
            sem((nz,)),
            sem((nz, n_br)),
            sem((nz, n_br)),
            sem((nz,)),
            sem((others,)),
        ],
        compiler_params=pltpu.CompilerParams(
            collective_id=0, has_side_effects=True, vmem_limit_bytes=52 * 1024 * 1024
        ),
        name="attention_backward",
    )(
        kv,
        resp_query,
        resp_grad_out,
        rnorm,
        rdelta,
        bias,
        response_key_rows,
        response_value_rows,
        prompt_query,
        prompt_grad_out,
        pnorm,
        pdelta,
    )
    return pdq, pdk, pdv, rdq, rdk, rdv


def solution(mesh):
    both = P("pre", "br")
    own = P(("pre", "br"), None)
    in_specs = (both,) * 6 + (own,) * 6 + (P(("pre", "br")),)
    out_specs = (both,) * 3 + (own,) * 3
    body = functools.partial(local, mesh.shape["pre"], mesh.shape["br"])
    return jax.shard_map(body, mesh=mesh, in_specs=in_specs, out_specs=out_specs, check_vma=False)
```
